128 devices in a mesh: dp: 4 (over y_hi, core), mp: 32 (over z, y_lo, x).
Axes of the slice: x: 4, y: 4 (y_hi: 2, y_lo: 2; y = y_hi * 2 + y_lo), z: 4, core: 2. Of those that a mesh axis runs over, the one named last changes fastest.
Arguments:
- pooled: bfloat16 [16384, 6144], P('dp', 'mp'), may hold values from -6 to 6
- proj: bfloat16 [6144, 1024], replicated, may hold values from -0.078125 to 0.078125
- text: bfloat16 [16384, 1024], P(('dp', 'mp')), may hold values from -0.1875 to 0.1875
- logit_scale: float32 [1], replicated, may hold values from 8 to 16
- logit_bias: float32 [1], replicated, may hold values from -6 to -4
Outputs:
- grad_text: float32 [16384, 1024], P(('dp', 'mp'))
- grad_proj: float32 [6144, 1024], P('mp')
The draws below stay inside these ranges and needn't reach their ends.
All inputs are finite; a program needn't handle non-finite values.
Results may differ from the reference program's by a relative error of at most 0.009.
Values may be sent and summed in bfloat16 or wider, within the bound.
A program may use at most 192 MiB of HBM per device.

```python
import jax
import jax.numpy as jnp
from jax import lax

E = 6144
P_SIZE = 1024
ROWS_DEV = 128
B = 16384
N_DP = 4
N_MP = 32


def block_scale(stream_key, shape, cuts, smallest, largest):
    gain, own = 1.0, jax.random.fold_in(stream_key, 6)
    for axis_at, blocks in cuts:
        draws = jnp.exp(jax.random.uniform(jax.random.fold_in(own, axis_at), (blocks,), jnp.float32, smallest / len(cuts), largest / len(cuts)))
        gain = gain * jnp.repeat(draws, shape[axis_at] // blocks).reshape([-1 if axis == axis_at else 1 for axis in range(len(shape))])
    return gain


def centred(own_key, extent, scale, most, cuts=(), kind=jnp.bfloat16):
    values = scale * jax.random.normal(own_key, extent, jnp.float32)
    if cuts:
        values = values * block_scale(own_key, extent, cuts, -0.22, 0.18)
    return jnp.clip(values, -most, most).astype(kind)


def setup_inputs(seed: int = 0) -> dict:
    key_list = jax.random.split(jax.random.key(seed), 6)
    pooled = centred(key_list[0], (B, E), 1.0, 6.0, ((0, 4), (1, 32)))
    proj = centred(key_list[1], (E, P_SIZE), E ** -0.5, 0.078125)
    text = centred(key_list[2], (B, P_SIZE), P_SIZE ** -0.5, 0.1875, ((0, 128),))
    logit_scale = jnp.clip(jax.random.uniform(key_list[3], (1,), jnp.float32, 8.0, 16.0), 8.0, 16.0)
    logit_bias = jnp.clip(jax.random.uniform(key_list[4], (1,), jnp.float32, -6.0, -4.0), -6.0, -4.0)
    return {"pooled": pooled, "proj": proj, "text": text, "logit_scale": logit_scale, "logit_bias": logit_bias}


EPS = 1e-06

def reference(pooled, proj, text, logit_scale, logit_bias):
    total = pooled.shape[0]
    group = ROWS_DEV * N_MP
    projected = jnp.dot(pooled, proj, preferred_element_type=jnp.float32)
    image_inverse = lax.rsqrt(lax.optimization_barrier(jnp.sum(projected * projected, axis=-1, keepdims=True)) + EPS)
    image_unit = (projected * image_inverse).astype(jnp.bfloat16)
    text_float = text.astype(jnp.float32)
    text_inverse = lax.rsqrt(lax.optimization_barrier(jnp.sum(text_float * text_float, axis=-1, keepdims=True)) + EPS)
    text_unit = (text_float * text_inverse).astype(jnp.bfloat16)
    scale = logit_scale[0]
    bias = logit_bias[0]
    columns = jnp.arange(total, dtype=jnp.int32)
    offsets = jnp.arange(group, dtype=jnp.int32)

    def block(carry, start):
        rows = lax.dynamic_slice_in_dim(image_unit, start, group, 0)
        logits = scale * jnp.dot(rows, text_unit.T, preferred_element_type=jnp.float32) + bias
        match = (start + offsets)[:, None] == columns[None, :]
        sign = jnp.where(match, jnp.float32(1.0), jnp.float32(-1.0))
        weights = (-sign * jax.nn.sigmoid(-sign * logits)).astype(jnp.bfloat16)
        rows_grad = scale * jnp.dot(weights, text_unit, preferred_element_type=jnp.float32)
        carry = carry + scale * jnp.dot(weights.T, rows, preferred_element_type=jnp.float32)
        return (carry, rows_grad)
    starts = jnp.arange(N_DP, dtype=jnp.int32) * group
    text_grad, image_blocks = lax.scan(block, jnp.zeros((total, proj.shape[1]), jnp.float32), starts)
    image_grad = image_blocks.reshape(total, proj.shape[1])
    unit_text = text_unit.astype(jnp.float32)
    grad_text = (text_grad - unit_text * lax.optimization_barrier(jnp.sum(unit_text * text_grad, axis=-1, keepdims=True))) * text_inverse
    unit_image = image_unit.astype(jnp.float32)
    delta = ((image_grad - unit_image * lax.optimization_barrier(jnp.sum(unit_image * image_grad, axis=-1, keepdims=True))) * image_inverse).astype(jnp.bfloat16)
    grad_proj = jnp.dot(pooled.T, delta, preferred_element_type=jnp.float32)
    return (grad_text, grad_proj)
```

```python
import functools

import jax
import jax.numpy as jnp
from jax import lax
from jax.experimental import pallas as pl
from jax.experimental.pallas import tpu as pltpu
from jax.sharding import PartitionSpec as P

EPS = 1e-06
LOG2E = 1.4426950408889634
MESH = pl.DeviceIdType.MESH
F32 = jnp.float32
BF16 = jnp.bfloat16
NT = (((1,), (1,)), ((), ()))
TN = (((0,), (0,)), ((), ()))
ROWS = 128
FEATS = 192
EMBED = 1024
HALF = EMBED // 2
MIRROR = [0, 1, 6, 7, 4, 5, 2, 3]
SEND_ORDER = [5, 2, 7, 4, 3, 6, 1]


def sems(*sizes):
    bases, total = [], 0
    for size in sizes:
        bases.append(total)
        total += size
    return bases, total


(S1, S2, TT, TC, IT, IR, DT, XC, XR, GC, GZ, GY, GF), N_SEMS = sems(
    32, 8, 9, 8, 9, 8, 9, 8, 8, 4, 4, 1, 1
)


def kernel(
    pooled_ref, proj_ref, text_ref, scale_ref, bias_ref, gtext_ref, gproj_ref,
    tile, rows_in, proj_v, images, texts, text_acc, img_out, img_in, deltas,
    core_out, core_in, text_out, text_in, gp, gp_out, gp_in, gz_out, gz_in,
    gy_out, gy_in, gf_out, gf_in, weights, send_sem, recv_sem, local_sem, proj_sem,
):
    dp = lax.axis_index("dp")
    mp = lax.axis_index("mp")
    core = dp % 2
    y = (dp // 2) * 2 + (mp // 4) % 2
    x = mp % 4
    z = mp // 8
    y_a = y + 1 - 2 * (y % 2)
    y_b = 3 - y

    def device(x_, y_, z_, core_):
        return ((y_ // 2) * 2 + core_, (z_ * 2 + y_ % 2) * 4 + x_)

    def image_peer(slot):
        return device((x + slot // 2) % 4, y_a if slot % 2 else y, z, core)

    def text_peer(slot):
        return device(x, y_b if slot % 2 else y, (z + slot // 2) % 4, core)

    partner = device(x, y, z, 1 - core)
    across = device(x, (y + 2) % 4, z, core)

    def position(slot):
        return (y_a if slot % 2 else y) % 2 * 4 + (x + slot // 2) % 4

    started = []

    def send(src, dst, sem_out, sem_in, to):
        copy = pltpu.make_async_remote_copy(
            src_ref=src, dst_ref=dst, send_sem=send_sem.at[sem_out],
            recv_sem=recv_sem.at[sem_in], device_id=to, device_id_type=MESH,
        )
        copy.start()
        started.append(copy)

    def arrived(dst, sem):
        pltpu.make_async_copy(dst, dst, recv_sem.at[sem]).wait()

    barrier = pltpu.get_barrier_semaphore()
    peers = [image_peer(s) for s in range(1, 8)] + [text_peer(s) for s in range(1, 8)]
    peers += [partner, across]
    for peer in peers:
        pl.semaphore_signal(barrier, inc=1, device_id=peer, device_id_type=MESH)

    proj_copies = []
    for slot in [MIRROR[s] for s in SEND_ORDER] + [0]:
        for k in range(4):
            shard = (z + k) % 4 * 8 + position(slot)
            copy = pltpu.make_async_copy(
                proj_ref.at[pl.ds(pl.multiple_of(shard * FEATS, FEATS), FEATS), :],
                proj_v.at[slot, pl.ds(k * FEATS, FEATS), :],
                proj_sem.at[slot, k],
            )
            copy.start()
            proj_copies.append((slot, copy))

    def block(ref, slot, rows=ROWS):
        return ref.at[pl.ds(slot * rows, rows), :]

    def part(k, slot):
        return tile.at[pl.ds(k * FEATS, FEATS), pl.ds(slot * ROWS, ROWS)]

    def shard_columns(dz, slot):
        start = (z + dz) % 4 * 1024 + position(slot) * ROWS
        return pooled_ref.at[:, pl.ds(pl.multiple_of(start, ROWS), ROWS)]

    pl.semaphore_wait(barrier, len(peers))

    local = []
    for slot in SEND_ORDER + [0]:
        for dz in (2, 1, 3):
            k = (4 - dz) % 4
            send(shard_columns(dz, slot), part(k, slot), S1 + dz * 8 + slot,
                 S1 + k * 8 + slot, text_peer(2 * dz))
        copy = pltpu.make_async_copy(shard_columns(0, slot), part(0, slot), local_sem.at[slot])
        copy.start()
        local.append((slot, copy))

    text_f = text_ref[...].astype(F32)
    text_inv = lax.rsqrt(jnp.sum(text_f * text_f, axis=-1, keepdims=True) + EPS)
    texts[0:ROWS, :] = (text_f * text_inv).astype(BF16)

    def to_core(slot):
        send(block(texts, slot), block(texts, 8 + slot), TC + slot, TC + slot, partner)

    def gather_1(ref, base, peer):
        send(block(ref, 0), block(ref, 1), base + 2, base + 2, peer(1))
        send(block(ref, 0), block(ref, 6), base + 0, base + 0, peer(2))
        send(block(ref, 0), block(ref, 2), base + 1, base + 1, peer(6))

    def gather_2(ref, base, peer):
        arrived(block(ref, 1), base + 2)
        send(block(ref, 1), block(ref, 7), base + 3, base + 3, peer(2))
        arrived(block(ref, 2), base + 1)
        send(block(ref, 2), block(ref, 4), base + 4, base + 4, peer(6))
        send(block(ref, 2), block(ref, 3), base + 5, base + 5, peer(1))
        arrived(block(ref, 6), base + 0)

    def piece(ref, slot, start, size):
        return ref.at[pl.ds(slot * ROWS + start, size), :]

    def gather_3(ref, base, peer):
        arrived(block(ref, 7), base + 3)
        send(piece(ref, 7, 0, 48), piece(ref, 5, 0, 48), base + 6, base + 6, peer(2))
        arrived(block(ref, 3), base + 5)
        send(piece(ref, 3, 48, 48), piece(ref, 5, 48, 48), base + 7, base + 7, peer(6))
        arrived(block(ref, 4), base + 4)
        send(piece(ref, 4, 96, 32), piece(ref, 5, 96, 32), base + 8, base + 8, peer(1))

    def gather_4(ref, base):
        arrived(piece(ref, 5, 0, 48), base + 6)
        arrived(piece(ref, 5, 48, 48), base + 7)
        arrived(piece(ref, 5, 96, 32), base + 8)

    to_core(0)

    for slot in SEND_ORDER + [0]:
        for k in (2, 1, 3):
            arrived(part(k, slot), S1 + k * 8 + slot)
        dict(local)[slot].wait()
        if slot:
            send(tile.at[:, pl.ds(slot * ROWS, ROWS)], rows_in.at[MIRROR[slot]],
                 S2 + slot, S2 + MIRROR[slot], image_peer(slot))

    gather_1(texts, TT, text_peer)

    projected = None
    for step, slot in enumerate([0] + [MIRROR[s] for s in SEND_ORDER]):
        if step == 4:
            gather_2(texts, TT, text_peer)
            for s in (1, 2, 6):
                to_core(s)
        for s, copy in proj_copies:
            if s == slot:
                copy.wait()
        if slot == 0:
            features = tile[:, 0:ROWS]
        else:
            arrived(rows_in.at[slot], S2 + slot)
            features = rows_in[slot]
        term = lax.dot_general(features, proj_v[slot], TN, preferred_element_type=F32)
        projected = term if projected is None else projected + term
    image_inv = lax.rsqrt(jnp.sum(projected * projected, axis=-1, keepdims=True) + EPS)
    images[0:ROWS, :] = (projected * image_inv).astype(BF16)
    gather_1(images, IT, image_peer)

    gather_3(texts, TT, text_peer)
    for s in (7, 3, 4):
        to_core(s)
    gather_2(images, IT, image_peer)
    gather_4(texts, TT)
    to_core(5)
    for s in range(8):
        arrived(block(texts, 8 + s), TC + s)

    scale = scale_ref[0]
    slope = -LOG2E * scale
    offset = -LOG2E * bias_ref[0]

    def pair(index, first):
        start = index * 2 * ROWS
        img = images[start:start + 2 * ROWS, :]
        power = slope * lax.dot_general(img, texts[...], NT, preferred_element_type=F32) + offset
        weights[...] = (1.0 / (1.0 + jnp.exp2(power))).astype(BF16)
        if index == 0:
            own = power[0:ROWS, 0:ROWS]
            match = (lax.broadcasted_iota(jnp.int32, (ROWS, ROWS), 0)
                     == lax.broadcasted_iota(jnp.int32, (ROWS, ROWS), 1))
            weights[0:ROWS, 0:ROWS] = jnp.where(
                match, -1.0 / (1.0 + jnp.exp2(-own)), 1.0 / (1.0 + jnp.exp2(own))
            ).astype(BF16)
        grad = scale * jnp.dot(weights[...], texts[...], preferred_element_type=F32)
        img_out[start:start + 2 * ROWS, :] = grad.astype(BF16)
        for slot in (2 * index + 1, 2 * index):
            if slot:
                send(block(img_out, slot), img_in.at[MIRROR[slot]], IR + slot,
                     IR + MIRROR[slot], image_peer(slot))
        term = lax.dot_general(weights[...], img, TN, preferred_element_type=F32)
        if first:
            text_acc[...] = term
        else:
            text_acc[...] += term
        return grad[0:ROWS, :]

    own_grad = pair(0, True)
    gather_3(images, IT, image_peer)
    pair(3, False)
    pair(1, False)
    gather_4(images, IT)
    pair(2, False)

    for s in range(8):
        core_out[s] = text_acc[(8 + s) * ROWS:(9 + s) * ROWS, :].astype(BF16)
        send(core_out.at[s], core_in.at[s], XC + s, XC + s, partner)
    for s in SEND_ORDER:
        arrived(core_in.at[s], XC + s)
        text_out[s] = (text_acc[s * ROWS:(s + 1) * ROWS, :] + core_in[s].astype(F32)).astype(BF16)
        send(text_out.at[s], text_in.at[MIRROR[s]], XR + s, XR + MIRROR[s], text_peer(s))

    grad = own_grad
    for s in range(1, 8):
        arrived(img_in.at[s], IR + s)
        grad = grad + img_in[s].astype(F32)
    unit = images[0:ROWS, :].astype(F32)
    deltas[0:ROWS, :] = (
        (grad - unit * jnp.sum(unit * grad, axis=-1, keepdims=True)) * image_inv
    ).astype(BF16)
    gather_1(deltas, DT, image_peer)
    gather_2(deltas, DT, image_peer)

    def term(index, k):
        cols = slice(index * 2 * ROWS, (index + 1) * 2 * ROWS)
        return jnp.dot(tile[k * FEATS:(k + 1) * FEATS, cols], deltas[cols, :],
                       preferred_element_type=F32)

    for k in range(4):
        gp[k] = term(0, k)
    gather_3(deltas, DT, image_peer)
    for k in range(4):
        gp[k] += term(3, k) + term(1, k)
    gather_4(deltas, DT)
    mine = pl.ds(pl.multiple_of(core * HALF, HALF), HALF)
    other = pl.ds(pl.multiple_of((1 - core) * HALF, HALF), HALF)
    for k in (2, 1, 3, 0):
        gp[k] += term(2, k)
        gp_out[k] = gp[k, :, other].astype(BF16)
        send(gp_out.at[k], gp_in.at[k], GC + k, GC + k, partner)
    for k in (2, 1, 3):
        arrived(gp_in.at[k], GC + k)
        gz_out[k] = (gp[k, :, mine] + gp_in[k].astype(F32)).astype(BF16)
        back = (4 - k) % 4
        send(gz_out.at[k], gz_in.at[back], GZ + k, GZ + back, text_peer(2 * k))
    arrived(gp_in.at[0], GC + 0)

    arrived(core_in.at[0], XC + 0)
    total = text_acc[0:ROWS, :] + core_in[0].astype(F32)
    for s in range(1, 8):
        arrived(text_in.at[s], XR + s)
        total = total + text_in[s].astype(F32)
    total = total * scale
    unit = texts[0:ROWS, :].astype(F32)
    gtext_ref[...] = (total - unit * jnp.sum(unit * total, axis=-1, keepdims=True)) * text_inv

    acc = gp[0, :, mine] + gp_in[0].astype(F32)
    for k in range(1, 4):
        arrived(gz_in.at[k], GZ + k)
        acc = acc + gz_in[k].astype(F32)
    gy_out[...] = acc.astype(BF16)
    send(gy_out, gy_in, GY, GY, across)
    arrived(gy_in, GY)
    gf_out[...] = gy_out[...].astype(F32) + gy_in[...].astype(F32)
    send(gf_out, gf_in, GF, GF, partner)
    gproj_ref[:, mine] = gf_out[...]
    arrived(gf_in, GF)
    gproj_ref[:, other] = gf_in[...]

    for copy in started:
        copy.wait_send()


def on_device(pooled, proj, text, logit_scale, logit_bias):
    vmem = pl.BlockSpec(memory_space=pltpu.VMEM)
    smem = pl.BlockSpec(memory_space=pltpu.SMEM)
    return pl.pallas_call(
        kernel,
        out_shape=(
            jax.ShapeDtypeStruct((ROWS, EMBED), F32),
            jax.ShapeDtypeStruct((FEATS, EMBED), F32),
        ),
        in_specs=[vmem, pl.BlockSpec(memory_space=pl.ANY), vmem, smem, smem],
        out_specs=(vmem, vmem),
        scratch_shapes=[
            pltpu.VMEM((4 * FEATS, 8 * ROWS), BF16),
            pltpu.VMEM((8, 4 * FEATS, ROWS), BF16),
            pltpu.VMEM((8, 4 * FEATS, EMBED), BF16),
            pltpu.VMEM((8 * ROWS, EMBED), BF16),
            pltpu.VMEM((16 * ROWS, EMBED), BF16),
            pltpu.VMEM((16 * ROWS, EMBED), F32),
            pltpu.VMEM((8 * ROWS, EMBED), BF16),
            pltpu.VMEM((8, ROWS, EMBED), BF16),
            pltpu.VMEM((8 * ROWS, EMBED), BF16),
            pltpu.VMEM((8, ROWS, EMBED), BF16),
            pltpu.VMEM((8, ROWS, EMBED), BF16),
            pltpu.VMEM((8, ROWS, EMBED), BF16),
            pltpu.VMEM((8, ROWS, EMBED), BF16),
            pltpu.VMEM((4, FEATS, EMBED), F32),
            pltpu.VMEM((4, FEATS, HALF), BF16),
            pltpu.VMEM((4, FEATS, HALF), BF16),
            pltpu.VMEM((4, FEATS, HALF), BF16),
            pltpu.VMEM((4, FEATS, HALF), BF16),
            pltpu.VMEM((FEATS, HALF), BF16),
            pltpu.VMEM((FEATS, HALF), BF16),
            pltpu.VMEM((FEATS, HALF), F32),
            pltpu.VMEM((FEATS, HALF), F32),
            pltpu.VMEM((2 * ROWS, 16 * ROWS), BF16),
            pltpu.SemaphoreType.DMA((N_SEMS,)),
            pltpu.SemaphoreType.DMA((N_SEMS,)),
            pltpu.SemaphoreType.DMA((8,)),
            pltpu.SemaphoreType.DMA((8, 4)),
        ],
        compiler_params=pltpu.CompilerParams(
            collective_id=0, has_side_effects=True, vmem_limit_bytes=63 * 2**20
        ),
    )(pooled.T, proj, text, logit_scale, logit_bias)


def solution(mesh):
    return jax.shard_map(
        on_device,
        mesh=mesh,
        in_specs=(P("dp", "mp"), P(), P(("dp", "mp"), None), P(), P()),
        out_specs=(P(("dp", "mp"), None), P("mp", None)),
        check_vma=False,
    )
```

```python
import functools

import jax
import jax.numpy as jnp
from jax import lax
from jax.experimental import pallas as pl
from jax.experimental.pallas import tpu as pltpu
from jax.sharding import PartitionSpec as P

EPS = 1e-06
LOG2E = 1.4426950408889634
MESH = pl.DeviceIdType.MESH
F32 = jnp.float32
BF16 = jnp.bfloat16
NT = (((1,), (1,)), ((), ()))
TN = (((0,), (0,)), ((), ()))
ROWS = 128
FEATS = 192
EMBED = 1024
HALF = EMBED // 2
QUARTER = EMBED // 4
OFFSETS = [(0, 0), (0, 1), (1, 0), (3, 0), (1, 1), (3, 1), (2, 0), (2, 1)]
MIRROR = [0, 1, 3, 2, 5, 4, 6, 7]
SEND_ORDER = [7,6,4,5,1,2,3]
BESIDE, NEXT, BACK = 1, 2, 3
AHEAD = 8
LAG = 4


def sems(*sizes):
    bases, total = [], 0
    for size in sizes:
        bases.append(total)
        total += size
    return bases, total


(S1, S2, TT, TC, IT, IR, DT, XC, XR, GC, GZ, GY, GF), N_SEMS = sems(
    32, 8, 9, 8, 9, 9, 18, 8, 9, 8, 8, 2, 2
)


def kernel(
    pooled_ref, proj_ref, text_ref, scale_ref, bias_ref, gtext_ref, gproj_ref,
    tile, rows_in, proj_v, images, texts, text_acc, img_out, img_in, deltas,
    core_out, core_in, text_out, text_in, gp, gp_out, gp_in, gz_out, gz_in,
    gy_out, gy_in, gf_out, gf_in, weights, send_sem, recv_sem, local_sem, proj_sem,
):
    dp = lax.axis_index("dp")
    mp = lax.axis_index("mp")
    core = dp % 2
    y = (dp // 2) * 2 + (mp // 4) % 2
    x = mp % 4
    z = mp // 8
    y_a = y + 1 - 2 * (y % 2)
    y_b = 3 - y

    def device(x_, y_, z_, core_):
        return ((y_ // 2) * 2 + core_, (z_ * 2 + y_ % 2) * 4 + x_)

    def image_peer(slot):
        steps, beside = OFFSETS[slot]
        return device((x + steps) % 4, y_a if beside else y, z, core)

    def text_peer(slot):
        steps, beside = OFFSETS[slot]
        return device(x, y_b if beside else y, (z + steps) % 4, core)

    def ring_peer(steps):
        return device(x, y, (z + steps) % 4, core)

    partner = device(x, y, z, 1 - core)
    across = device(x, (y + 2) % 4, z, core)

    def position(slot):
        steps, beside = OFFSETS[slot]
        return (y_a if beside else y) % 2 * 4 + (x + steps) % 4

    started = []

    def send(src, dst, sem_out, sem_in, to):
        copy = pltpu.make_async_remote_copy(
            src_ref=src, dst_ref=dst, send_sem=send_sem.at[sem_out],
            recv_sem=recv_sem.at[sem_in], device_id=to, device_id_type=MESH,
        )
        copy.start()
        started.append(copy)

    def arrived(dst, sem):
        pltpu.make_async_copy(dst, dst, recv_sem.at[sem]).wait()

    barrier = pltpu.get_barrier_semaphore()
    peers = [image_peer(s) for s in range(1, 8)] + [text_peer(s) for s in range(1, 8)]
    peers += [partner, across]
    for peer in peers:
        pl.semaphore_signal(barrier, inc=1, device_id=peer, device_id_type=MESH)

    whole = slice(None)

    def block(ref, slot, cols=whole):
        return ref.at[pl.ds(slot * ROWS, ROWS), cols]

    def part(k, slot):
        return tile.at[pl.ds(k * FEATS, FEATS), pl.ds(slot * ROWS, ROWS)]

    def shard_columns(dz, slot):
        start = (z + dz) % 4 * 1024 + position(slot) * ROWS
        return pooled_ref.at[:, pl.ds(pl.multiple_of(start, ROWS), ROWS)]

    pl.semaphore_wait(barrier, len(peers))

    order = SEND_ORDER + [0]
    local = {}

    def first_stage(slot):
        for dz in (2, 1, 3):
            k = (4 - dz) % 4
            send(shard_columns(dz, slot), part(k, slot), S1 + dz * 8 + slot,
                 S1 + k * 8 + slot, ring_peer(dz))
        local[slot] = pltpu.make_async_copy(
            shard_columns(0, slot), part(0, slot), local_sem.at[slot])
        local[slot].start()

    for slot in order[:AHEAD]:
        first_stage(slot)

    proj_copies = []
    for slot in [MIRROR[s] for s in SEND_ORDER] + [0]:
        for k in range(4):
            shard = (z + k) % 4 * 8 + position(slot)
            copy = pltpu.make_async_copy(
                proj_ref.at[pl.ds(pl.multiple_of(shard * FEATS, FEATS), FEATS), :],
                proj_v.at[slot, pl.ds(k * FEATS, FEATS), :],
                proj_sem.at[slot, k],
            )
            copy.start()
            proj_copies.append((slot, copy))

    text_f = text_ref[...].astype(F32)
    text_inv = lax.rsqrt(jnp.sum(text_f * text_f, axis=-1, keepdims=True) + EPS)
    texts[0:ROWS, :] = (text_f * text_inv).astype(BF16)

    def to_core(slot):
        send(block(texts, slot), block(texts, 8 + slot), TC + slot, TC + slot, partner)

    def piece(ref, slot, start, size, cols=whole):
        return ref.at[pl.ds(slot * ROWS + start, size), cols]

    def gather_1(ref, base, peer, cols=whole):
        send(block(ref, 0, cols), block(ref, 1, cols), base + 0, base + 0, peer(BESIDE))
        send(block(ref, 0, cols), block(ref, 3, cols), base + 1, base + 1, peer(NEXT))
        send(block(ref, 0, cols), block(ref, 2, cols), base + 2, base + 2, peer(BACK))

    def gather_2(ref, base, peer, cols=whole):
        arrived(block(ref, 1, cols), base + 0)
        send(block(ref, 1, cols), block(ref, 5, cols), base + 3, base + 3, peer(NEXT))
        arrived(block(ref, 2, cols), base + 2)
        send(block(ref, 2, cols), block(ref, 6, cols), base + 4, base + 4, peer(BACK))
        send(block(ref, 2, cols), block(ref, 4, cols), base + 5, base + 5, peer(BESIDE))
        arrived(block(ref, 3, cols), base + 1)

    def gather_3(ref, base, peer, cols=whole):
        arrived(block(ref, 5, cols), base + 3)
        send(piece(ref, 5, 0, 48, cols), piece(ref, 7, 0, 48, cols), base + 6, base + 6, peer(NEXT))
        arrived(block(ref, 4, cols), base + 5)
        send(piece(ref, 4, 48, 48, cols), piece(ref, 7, 48, 48, cols), base + 7, base + 7, peer(BACK))
        arrived(block(ref, 6, cols), base + 4)
        send(piece(ref, 6, 96, 32, cols), piece(ref, 7, 96, 32, cols), base + 8, base + 8, peer(BESIDE))

    def gather_4(ref, base, cols=whole):
        arrived(piece(ref, 7, 0, 48, cols), base + 6)
        arrived(piece(ref, 7, 48, 48, cols), base + 7)
        arrived(piece(ref, 7, 96, 32, cols), base + 8)

    def reduce_1(ref, ref_in, base, peer):
        send(piece(ref, 7, 0, 48), piece(ref_in, 7, 0, 48), base + 6, base + 6, peer(BACK))
        send(piece(ref, 7, 48, 48), piece(ref_in, 7, 48, 48), base + 7, base + 7, peer(NEXT))
        send(piece(ref, 7, 96, 32), piece(ref_in, 7, 96, 32), base + 8, base + 8, peer(BESIDE))

    def reduce_2(slot, ref, ref_in, base, peer, own):
        start, size, sem, at, towards = {
            5: (0, 48, 6, 3, BACK), 4: (48, 48, 7, 5, BESIDE), 6: (96, 32, 8, 4, NEXT)
        }[slot]
        arrived(piece(ref_in, 7, start, size), base + sem)
        ref[slot * ROWS:(slot + 1) * ROWS, :] = own(slot).astype(BF16)
        rows = slice(slot * ROWS + start, slot * ROWS + start + size)
        part_in = ref_in[7 * ROWS + start:7 * ROWS + start + size, :].astype(F32)
        ref[rows, :] = (own(slot)[start:start + size, :] + part_in).astype(BF16)
        send(block(ref, slot), block(ref_in, slot), base + at, base + at, peer(towards))

    def reduce_3(slot, ref, ref_in, base, peer, own):
        total = own(slot)
        for at, sem in {1: [(5, 3)], 2: [(6, 4), (4, 5)], 3: []}[slot]:
            arrived(block(ref_in, at), base + sem)
            total = total + ref_in[at * ROWS:(at + 1) * ROWS, :].astype(F32)
        ref[slot * ROWS:(slot + 1) * ROWS, :] = total.astype(BF16)
        send(block(ref, slot), block(ref_in, slot), base + slot - 1, base + slot - 1, peer(slot))

    def reduce_4(total, ref_in, base):
        for slot in (1, 2, 3):
            arrived(block(ref_in, slot), base + slot - 1)
            total = total + ref_in[slot * ROWS:(slot + 1) * ROWS, :].astype(F32)
        return total

    to_core(0)

    def project(slot):
        for s, copy in proj_copies:
            if s == slot:
                copy.wait()
        if slot:
            arrived(rows_in.at[slot], S2 + slot)
        features = rows_in[slot] if slot else tile[:, 0:ROWS]
        return lax.dot_general(features, proj_v[slot], TN, preferred_element_type=F32)

    projected = jnp.zeros((ROWS, EMBED), F32)
    for step, slot in enumerate(order):
        for k in (2, 1, 3):
            arrived(part(k, slot), S1 + k * 8 + slot)
        local[slot].wait()
        if step + AHEAD < 8:
            first_stage(order[step + AHEAD])
        if slot:
            send(tile.at[:, pl.ds(slot * ROWS, ROWS)], rows_in.at[MIRROR[slot]],
                 S2 + slot, S2 + MIRROR[slot], image_peer(slot))
        if step >= LAG:
            projected = projected + project(MIRROR[order[step - LAG]])
        if step == 5:
            gather_1(texts, TT, text_peer)
    projected = projected + project(0)
    for slot in order[8 - LAG:7]:
        projected = projected + project(MIRROR[slot])
        if slot == order[5]:
            gather_2(texts, TT, text_peer)
            for s in (1, 2, 3):
                to_core(s)
    image_inv = lax.rsqrt(jnp.sum(projected * projected, axis=-1, keepdims=True) + EPS)
    images[0:ROWS, :] = (projected * image_inv).astype(BF16)
    gather_1(images, IT, image_peer)

    gather_3(texts, TT, text_peer)
    for s in (4, 5, 6):
        to_core(s)
    gather_2(images, IT, image_peer)
    gather_4(texts, TT)
    to_core(7)
    for s in range(8):
        arrived(block(texts, 8 + s), TC + s)

    scale = scale_ref[0]
    slope = -LOG2E * scale
    offset = -LOG2E * bias_ref[0]

    def pair(index):
        start = index * 2 * ROWS
        rows = slice(start, start + 2 * ROWS)
        power = slope * lax.dot_general(
            images[rows, :], texts[...], NT, preferred_element_type=F32) + offset
        weights[rows, :] = (1.0 / (1.0 + jnp.exp2(power))).astype(BF16)
        if index == 0:
            own = power[0:ROWS, 0:ROWS]
            match = (lax.broadcasted_iota(jnp.int32, (ROWS, ROWS), 0)
                     == lax.broadcasted_iota(jnp.int32, (ROWS, ROWS), 1))
            weights[0:ROWS, 0:ROWS] = jnp.where(
                match, -1.0 / (1.0 + jnp.exp2(-own)), 1.0 / (1.0 + jnp.exp2(own))
            ).astype(BF16)
        grad = jnp.dot(weights[rows, :], texts[...], preferred_element_type=F32)
        img_out[rows, :] = grad.astype(BF16)
        return grad[0:ROWS, :]

    def text_term(first, last):
        rows = slice(first * 2 * ROWS, (last + 1) * 2 * ROWS)
        return lax.dot_general(
            weights[rows, :], images[rows, :], TN, preferred_element_type=F32)

    def image_part(slot):
        return img_out[slot * ROWS:(slot + 1) * ROWS, :].astype(F32)

    images_tree = (img_out, img_in, IR, image_peer, image_part)
    own_grad = pair(0)
    gather_3(images, IT, image_peer)
    pair(1)
    text_acc[...] = text_term(0, 1)
    gather_4(images, IT)
    pair(3)
    reduce_1(img_out, img_in, IR, image_peer)
    pair(2)
    for s in (5, 4, 6):
        reduce_2(s, *images_tree)
    reduce_3(3, *images_tree)
    text_acc[...] += text_term(2, 3)

    for s in (7, 5, 4, 6, 1, 2, 3, 0):
        core_out[s] = text_acc[(8 + s) * ROWS:(9 + s) * ROWS, :].astype(BF16)
        send(core_out.at[s], core_in.at[s], XC + s, XC + s, partner)

    def text_part(slot):
        return text_acc[slot * ROWS:(slot + 1) * ROWS, :] + core_in[slot].astype(F32)

    texts_tree = (text_out, text_in, XR, text_peer, text_part)
    reduce_3(1, *images_tree)
    reduce_3(2, *images_tree)
    arrived(core_in.at[7], XC + 7)
    text_out[7 * ROWS:8 * ROWS, :] = text_part(7).astype(BF16)
    reduce_1(text_out, text_in, XR, text_peer)
    for s in (5, 4, 6):
        arrived(core_in.at[s], XC + s)
        reduce_2(s, *texts_tree)
    arrived(core_in.at[3], XC + 3)
    reduce_3(3, *texts_tree)

    grad = reduce_4(own_grad, img_in, IR)
    unit = images[0:ROWS, :].astype(F32)
    deltas[0:ROWS, :] = (
        (grad - unit * jnp.sum(unit * grad, axis=-1, keepdims=True)) * image_inv
    ).astype(BF16)
    cols = [pl.ds(0, HALF), pl.ds(HALF, HALF)]
    mine = pl.ds(pl.multiple_of(core * QUARTER, QUARTER), QUARTER)
    other = pl.ds(pl.multiple_of((1 - core) * QUARTER, QUARTER), QUARTER)

    def place(half, which):
        return pl.ds(pl.multiple_of(half * HALF + which * QUARTER, QUARTER), QUARTER)

    def multiply(h):
        for k in (2, 1, 3, 0):
            gp[h, k] = jnp.dot(tile[k * FEATS:(k + 1) * FEATS, :], deltas[:, h * HALF:(h + 1) * HALF],
                               preferred_element_type=F32)
            gp_out[h, k] = gp[h, k, :, other].astype(BF16)
            send(gp_out.at[h, k], gp_in.at[h, k], GC + 4 * h + k, GC + 4 * h + k, partner)

    def along_z(h):
        for k in (2, 1, 3):
            arrived(gp_in.at[h, k], GC + 4 * h + k)
            gz_out[h, k] = (gp[h, k, :, mine] + gp_in[h, k].astype(F32)).astype(BF16)
            back = (4 - k) % 4
            send(gz_out.at[h, k], gz_in.at[h, back], GZ + 4 * h + k, GZ + 4 * h + back, ring_peer(k))

    def along_y(h):
        arrived(gp_in.at[h, 0], GC + 4 * h)
        acc = gp[h, 0, :, mine] + gp_in[h, 0].astype(F32)
        for k in range(1, 4):
            arrived(gz_in.at[h, k], GZ + 4 * h + k)
            acc = acc + gz_in[h, k].astype(F32)
        gy_out[h] = acc.astype(BF16)
        send(gy_out.at[h], gy_in.at[h], GY + h, GY + h, across)

    def to_partner(h):
        arrived(gy_in.at[h], GY + h)
        gf_out[h] = gy_out[h].astype(F32) + gy_in[h].astype(F32)
        send(gf_out.at[h], gf_in.at[h], GF + h, GF + h, partner)
        gproj_ref[:, place(h, core)] = gf_out[h]

    def finish(h):
        arrived(gf_in.at[h], GF + h)
        gproj_ref[:, place(h, 1 - core)] = gf_in[h]

    gather_1(deltas, DT, image_peer, cols[0])
    for s in (1, 2):
        arrived(core_in.at[s], XC + s)
        reduce_3(s, *texts_tree)
    gather_2(deltas, DT, image_peer, cols[0])
    gather_1(deltas, DT + 9, image_peer, cols[1])
    gather_3(deltas, DT, image_peer, cols[0])
    gather_2(deltas, DT + 9, image_peer, cols[1])
    gather_4(deltas, DT, cols[0])
    multiply(0)
    gather_3(deltas, DT + 9, image_peer, cols[1])
    along_z(0)
    gather_4(deltas, DT + 9, cols[1])
    multiply(1)
    along_y(0)
    along_z(1)

    arrived(core_in.at[0], XC + 0)
    total = reduce_4(text_part(0), text_in, XR)
    unit = texts[0:ROWS, :].astype(F32)
    gtext_ref[...] = (total - unit * jnp.sum(unit * total, axis=-1, keepdims=True)) * text_inv
    to_partner(0)
    along_y(1)
    finish(0)
    to_partner(1)
    finish(1)

    for copy in started:
        copy.wait_send()


def on_device(pooled, proj, text, logit_scale, logit_bias):
    vmem = pl.BlockSpec(memory_space=pltpu.VMEM)
    smem = pl.BlockSpec(memory_space=pltpu.SMEM)
    grad_text, grad_proj = pl.pallas_call(
        kernel,
        out_shape=(
            jax.ShapeDtypeStruct((ROWS, EMBED), F32),
            jax.ShapeDtypeStruct((FEATS, EMBED), F32),
        ),
        in_specs=[vmem, pl.BlockSpec(memory_space=pl.ANY), vmem, smem, smem],
        out_specs=(vmem, vmem),
        scratch_shapes=[
            pltpu.VMEM((4 * FEATS, 8 * ROWS), BF16),
            pltpu.VMEM((8, 4 * FEATS, ROWS), BF16),
            pltpu.VMEM((8, 4 * FEATS, EMBED), BF16),
            pltpu.VMEM((8 * ROWS, EMBED), BF16),
            pltpu.VMEM((16 * ROWS, EMBED), BF16),
            pltpu.VMEM((16 * ROWS, EMBED), F32),
            pltpu.VMEM((8 * ROWS, EMBED), BF16),
            pltpu.VMEM((8 * ROWS, EMBED), BF16),
            pltpu.VMEM((8 * ROWS, EMBED), BF16),
            pltpu.VMEM((8, ROWS, EMBED), BF16),
            pltpu.VMEM((8, ROWS, EMBED), BF16),
            pltpu.VMEM((8 * ROWS, EMBED), BF16),
            pltpu.VMEM((8 * ROWS, EMBED), BF16),
            pltpu.VMEM((2, 4, FEATS, HALF), F32),
            pltpu.VMEM((2, 4, FEATS, QUARTER), BF16),
            pltpu.VMEM((2, 4, FEATS, QUARTER), BF16),
            pltpu.VMEM((2, 4, FEATS, QUARTER), BF16),
            pltpu.VMEM((2, 4, FEATS, QUARTER), BF16),
            pltpu.VMEM((2, FEATS, QUARTER), BF16),
            pltpu.VMEM((2, FEATS, QUARTER), BF16),
            pltpu.VMEM((2, FEATS, QUARTER), F32),
            pltpu.VMEM((2, FEATS, QUARTER), F32),
            pltpu.VMEM((8 * ROWS, 16 * ROWS), BF16),
            pltpu.SemaphoreType.DMA((N_SEMS,)),
            pltpu.SemaphoreType.DMA((N_SEMS,)),
            pltpu.SemaphoreType.DMA((8,)),
            pltpu.SemaphoreType.DMA((8, 4)),
        ],
        compiler_params=pltpu.CompilerParams(
            collective_id=0, has_side_effects=True, vmem_limit_bytes=63 * 2**20
        ),
    )(pooled.T, proj, text, logit_scale, logit_bias)
    return (logit_scale[0] * grad_text, logit_scale[0] * grad_proj)


def solution(mesh):
    return jax.shard_map(
        on_device,
        mesh=mesh,
        in_specs=(P("dp", "mp"), P(), P(("dp", "mp"), None), P(), P()),
        out_specs=(P(("dp", "mp"), None), P("mp", None)),
        check_vma=False,
    )
```

```python
import functools

import jax
import jax.numpy as jnp
from jax import lax
from jax.experimental import pallas as pl
from jax.experimental.pallas import tpu as pltpu
from jax.sharding import PartitionSpec as P

EPS = 1e-06
LOG2E = 1.4426950408889634
MESH = pl.DeviceIdType.MESH
F32 = jnp.float32
BF16 = jnp.bfloat16
NT = (((1,), (1,)), ((), ()))
TN = (((0,), (0,)), ((), ()))
ROWS = 128
FEATS = 192
EMBED = 1024
HALF = EMBED // 2
QUARTER = EMBED // 4
OFFSETS = [(0, 0), (0, 1), (1, 0), (3, 0), (1, 1), (3, 1), (2, 0), (2, 1)]
MIRROR = [0, 1, 3, 2, 5, 4, 6, 7]
SEND_ORDER = [7,6,4,5,1,2,3]
BESIDE, NEXT, BACK = 1, 2, 3
AHEAD = 8
LAG = 4


def sems(*sizes):
    bases, total = [], 0
    for size in sizes:
        bases.append(total)
        total += size
    return bases, total


(S1, S2, TT, TC, IT, IR, DT, XC, XR, GC, GZ, GY, GF), N_SEMS = sems(
    32, 8, 9, 8, 9, 9, 18, 8, 9, 8, 8, 2, 2
)


def kernel(
    pooled_ref, proj_ref, text_ref, scale_ref, bias_ref, gtext_ref, gproj_ref,
    tile, rows_in, proj_v, images, texts, text_acc, img_out, img_in, deltas,
    core_out, core_in, text_out, text_in, gp, gp_out, gp_in, gz_out, gz_in,
    gy_out, gy_in, gf_out, gf_in, weights, send_sem, recv_sem, local_sem, proj_sem,
):
    dp = lax.axis_index("dp")
    mp = lax.axis_index("mp")
    core = dp % 2
    y = (dp // 2) * 2 + (mp // 4) % 2
    x = mp % 4
    z = mp // 8
    y_a = y + 1 - 2 * (y % 2)
    y_b = 3 - y

    def device(x_, y_, z_, core_):
        return ((y_ // 2) * 2 + core_, (z_ * 2 + y_ % 2) * 4 + x_)

    def image_peer(slot):
        steps, beside = OFFSETS[slot]
        return device((x + steps) % 4, y_a if beside else y, z, core)

    def text_peer(slot):
        steps, beside = OFFSETS[slot]
        return device(x, y_b if beside else y, (z + steps) % 4, core)

    def ring_peer(steps):
        return device(x, y, (z + steps) % 4, core)

    partner = device(x, y, z, 1 - core)
    across = device(x, (y + 2) % 4, z, core)

    def position(slot):
        steps, beside = OFFSETS[slot]
        return (y_a if beside else y) % 2 * 4 + (x + steps) % 4

    started = []

    def send(src, dst, sem_out, sem_in, to):
        copy = pltpu.make_async_remote_copy(
            src_ref=src, dst_ref=dst, send_sem=send_sem.at[sem_out],
            recv_sem=recv_sem.at[sem_in], device_id=to, device_id_type=MESH,
        )
        copy.start()
        started.append(copy)

    def arrived(dst, sem):
        pltpu.make_async_copy(dst, dst, recv_sem.at[sem]).wait()

    barrier = pltpu.get_barrier_semaphore()
    peers = [image_peer(s) for s in range(1, 8)] + [text_peer(s) for s in range(1, 8)]
    peers += [partner, across]
    for peer in peers:
        pl.semaphore_signal(barrier, inc=1, device_id=peer, device_id_type=MESH)

    whole = slice(None)

    def block(ref, slot, cols=whole):
        return ref.at[pl.ds(slot * ROWS, ROWS), cols]

    def part(k, slot):
        return tile.at[pl.ds(k * FEATS, FEATS), pl.ds(slot * ROWS, ROWS)]

    def shard_columns(dz, slot):
        start = (z + dz) % 4 * 1024 + position(slot) * ROWS
        return pooled_ref.at[:, pl.ds(pl.multiple_of(start, ROWS), ROWS)]

    pl.semaphore_wait(barrier, len(peers))

    order = SEND_ORDER + [0]
    local = {}

    def first_stage(slot):
        for dz in (2, 1, 3):
            k = (4 - dz) % 4
            send(shard_columns(dz, slot), part(k, slot), S1 + dz * 8 + slot,
                 S1 + k * 8 + slot, ring_peer(dz))
        local[slot] = pltpu.make_async_copy(
            shard_columns(0, slot), part(0, slot), local_sem.at[slot])
        local[slot].start()

    for slot in order[:AHEAD]:
        first_stage(slot)

    proj_copies = []
    for slot in [MIRROR[s] for s in SEND_ORDER] + [0]:
        for k in range(4):
            shard = (z + k) % 4 * 8 + position(slot)
            copy = pltpu.make_async_copy(
                proj_ref.at[pl.ds(pl.multiple_of(shard * FEATS, FEATS), FEATS), :],
                proj_v.at[slot, pl.ds(k * FEATS, FEATS), :],
                proj_sem.at[slot, k],
            )
            copy.start()
            proj_copies.append((slot, copy))

    text_f = text_ref[...].astype(F32)
    text_inv = lax.rsqrt(jnp.sum(text_f * text_f, axis=-1, keepdims=True) + EPS)
    texts[0:ROWS, :] = (text_f * text_inv).astype(BF16)

    def to_core(slot):
        send(block(texts, slot), block(texts, 8 + slot), TC + slot, TC + slot, partner)

    def piece(ref, slot, start, size, cols=whole):
        return ref.at[pl.ds(slot * ROWS + start, size), cols]

    def gather_1(ref, base, peer, cols=whole):
        send(block(ref, 0, cols), block(ref, 1, cols), base + 0, base + 0, peer(BESIDE))
        send(block(ref, 0, cols), block(ref, 3, cols), base + 1, base + 1, peer(NEXT))
        send(block(ref, 0, cols), block(ref, 2, cols), base + 2, base + 2, peer(BACK))

    def gather_2(ref, base, peer, cols=whole):
        arrived(block(ref, 1, cols), base + 0)
        send(block(ref, 1, cols), block(ref, 5, cols), base + 3, base + 3, peer(NEXT))
        arrived(block(ref, 2, cols), base + 2)
        send(block(ref, 2, cols), block(ref, 6, cols), base + 4, base + 4, peer(BACK))
        send(block(ref, 2, cols), block(ref, 4, cols), base + 5, base + 5, peer(BESIDE))
        arrived(block(ref, 3, cols), base + 1)

    def gather_3(ref, base, peer, cols=whole):
        arrived(block(ref, 5, cols), base + 3)
        send(piece(ref, 5, 0, 48, cols), piece(ref, 7, 0, 48, cols), base + 6, base + 6, peer(NEXT))
        arrived(block(ref, 4, cols), base + 5)
        send(piece(ref, 4, 48, 48, cols), piece(ref, 7, 48, 48, cols), base + 7, base + 7, peer(BACK))
        arrived(block(ref, 6, cols), base + 4)
        send(piece(ref, 6, 96, 32, cols), piece(ref, 7, 96, 32, cols), base + 8, base + 8, peer(BESIDE))

    def gather_4(ref, base, cols=whole):
        arrived(piece(ref, 7, 0, 48, cols), base + 6)
        arrived(piece(ref, 7, 48, 48, cols), base + 7)
        arrived(piece(ref, 7, 96, 32, cols), base + 8)

    def reduce_1(ref, ref_in, base, peer):
        send(piece(ref, 7, 0, 48), piece(ref_in, 7, 0, 48), base + 6, base + 6, peer(BACK))
        send(piece(ref, 7, 48, 48), piece(ref_in, 7, 48, 48), base + 7, base + 7, peer(NEXT))
        send(piece(ref, 7, 96, 32), piece(ref_in, 7, 96, 32), base + 8, base + 8, peer(BESIDE))

    def reduce_2(slot, ref, ref_in, base, peer, own):
        start, size, sem, at, towards = {
            5: (0, 48, 6, 3, BACK), 4: (48, 48, 7, 5, BESIDE), 6: (96, 32, 8, 4, NEXT)
        }[slot]
        arrived(piece(ref_in, 7, start, size), base + sem)
        ref[slot * ROWS:(slot + 1) * ROWS, :] = own(slot).astype(BF16)
        rows = slice(slot * ROWS + start, slot * ROWS + start + size)
        part_in = ref_in[7 * ROWS + start:7 * ROWS + start + size, :].astype(F32)
        ref[rows, :] = (own(slot)[start:start + size, :] + part_in).astype(BF16)
        send(block(ref, slot), block(ref_in, slot), base + at, base + at, peer(towards))

    def reduce_3(slot, ref, ref_in, base, peer, own):
        total = own(slot)
        for at, sem in {1: [(5, 3)], 2: [(6, 4), (4, 5)], 3: []}[slot]:
            arrived(block(ref_in, at), base + sem)
            total = total + ref_in[at * ROWS:(at + 1) * ROWS, :].astype(F32)
        ref[slot * ROWS:(slot + 1) * ROWS, :] = total.astype(BF16)
        send(block(ref, slot), block(ref_in, slot), base + slot - 1, base + slot - 1, peer(slot))

    def reduce_4(total, ref_in, base):
        for slot in (1, 2, 3):
            arrived(block(ref_in, slot), base + slot - 1)
            total = total + ref_in[slot * ROWS:(slot + 1) * ROWS, :].astype(F32)
        return total

    def project(slot):
        for s, copy in proj_copies:
            if s == slot:
                copy.wait()
        if slot:
            arrived(rows_in.at[slot], S2 + slot)
        features = rows_in[slot] if slot else tile[:, 0:ROWS]
        return lax.dot_general(features, proj_v[slot], TN, preferred_element_type=F32)

    projected = jnp.zeros((ROWS, EMBED), F32)
    for step, slot in enumerate(order):
        for k in (2, 1, 3):
            arrived(part(k, slot), S1 + k * 8 + slot)
        local[slot].wait()
        if step + AHEAD < 8:
            first_stage(order[step + AHEAD])
        if slot:
            send(tile.at[:, pl.ds(slot * ROWS, ROWS)], rows_in.at[MIRROR[slot]],
                 S2 + slot, S2 + MIRROR[slot], image_peer(slot))
        if step >= LAG:
            projected = projected + project(MIRROR[order[step - LAG]])
        if step == 5:
            gather_1(texts, TT, text_peer)
            to_core(0)
    projected = projected + project(0)
    for slot in order[8 - LAG:7]:
        projected = projected + project(MIRROR[slot])
        if slot == order[5]:
            gather_2(texts, TT, text_peer)
            for s in (1, 2, 3):
                to_core(s)
    image_inv = lax.rsqrt(jnp.sum(projected * projected, axis=-1, keepdims=True) + EPS)
    images[0:ROWS, :] = (projected * image_inv).astype(BF16)
    gather_1(images, IT, image_peer)

    gather_3(texts, TT, text_peer)
    for s in (4, 5, 6):
        to_core(s)
    gather_2(images, IT, image_peer)
    gather_4(texts, TT)
    to_core(7)
    for s in range(8):
        arrived(block(texts, 8 + s), TC + s)

    scale = scale_ref[0]
    slope = -LOG2E * scale
    offset = -LOG2E * bias_ref[0]

    def pair(index):
        start = index * 2 * ROWS
        rows = slice(start, start + 2 * ROWS)
        power = slope * lax.dot_general(
            images[rows, :], texts[...], NT, preferred_element_type=F32) + offset
        weights[rows, :] = (1.0 / (1.0 + jnp.exp2(power))).astype(BF16)
        if index == 0:
            own = power[0:ROWS, 0:ROWS]
            match = (lax.broadcasted_iota(jnp.int32, (ROWS, ROWS), 0)
                     == lax.broadcasted_iota(jnp.int32, (ROWS, ROWS), 1))
            weights[0:ROWS, 0:ROWS] = jnp.where(
                match, -1.0 / (1.0 + jnp.exp2(-own)), 1.0 / (1.0 + jnp.exp2(own))
            ).astype(BF16)
        grad = jnp.dot(weights[rows, :], texts[...], preferred_element_type=F32)
        img_out[rows, :] = grad.astype(BF16)
        return grad[0:ROWS, :]

    def text_term(first, last):
        rows = slice(first * 2 * ROWS, (last + 1) * 2 * ROWS)
        return lax.dot_general(
            weights[rows, :], images[rows, :], TN, preferred_element_type=F32)

    def image_part(slot):
        return img_out[slot * ROWS:(slot + 1) * ROWS, :].astype(F32)

    images_tree = (img_out, img_in, IR, image_peer, image_part)
    own_grad = pair(0)
    pair(1)
    text_acc[...] = text_term(0, 1)
    gather_3(images, IT, image_peer)
    pair(2)
    gather_4(images, IT)
    pair(3)
    reduce_1(img_out, img_in, IR, image_peer)
    text_acc[...] += text_term(2, 3)
    for s in (5, 4, 6):
        reduce_2(s, *images_tree)
    reduce_3(3, *images_tree)

    for s in (7, 5, 4, 6, 1, 2, 3, 0):
        core_out[s] = text_acc[(8 + s) * ROWS:(9 + s) * ROWS, :].astype(BF16)
        send(core_out.at[s], core_in.at[s], XC + s, XC + s, partner)

    def text_part(slot):
        return text_acc[slot * ROWS:(slot + 1) * ROWS, :] + core_in[slot].astype(F32)

    texts_tree = (text_out, text_in, XR, text_peer, text_part)
    reduce_3(1, *images_tree)
    reduce_3(2, *images_tree)
    arrived(core_in.at[7], XC + 7)
    text_out[7 * ROWS:8 * ROWS, :] = text_part(7).astype(BF16)
    reduce_1(text_out, text_in, XR, text_peer)
    for s in (5, 4, 6):
        arrived(core_in.at[s], XC + s)
        reduce_2(s, *texts_tree)
    arrived(core_in.at[3], XC + 3)
    reduce_3(3, *texts_tree)

    grad = reduce_4(own_grad, img_in, IR)
    unit = images[0:ROWS, :].astype(F32)
    deltas[0:ROWS, :] = (
        (grad - unit * jnp.sum(unit * grad, axis=-1, keepdims=True)) * image_inv
    ).astype(BF16)
    cols = [pl.ds(0, HALF), pl.ds(HALF, HALF)]
    mine = pl.ds(pl.multiple_of(core * QUARTER, QUARTER), QUARTER)
    other = pl.ds(pl.multiple_of((1 - core) * QUARTER, QUARTER), QUARTER)

    def place(half, which):
        return pl.ds(pl.multiple_of(half * HALF + which * QUARTER, QUARTER), QUARTER)

    def multiply(h):
        for k in (2, 1, 3, 0):
            gp[h, k] = jnp.dot(tile[k * FEATS:(k + 1) * FEATS, :], deltas[:, h * HALF:(h + 1) * HALF],
                               preferred_element_type=F32)
            gp_out[h, k] = gp[h, k, :, other].astype(BF16)
            send(gp_out.at[h, k], gp_in.at[h, k], GC + 4 * h + k, GC + 4 * h + k, partner)

    def along_z(h):
        for k in (2, 1, 3):
            arrived(gp_in.at[h, k], GC + 4 * h + k)
            gz_out[h, k] = (gp[h, k, :, mine] + gp_in[h, k].astype(F32)).astype(BF16)
            back = (4 - k) % 4
            send(gz_out.at[h, k], gz_in.at[h, back], GZ + 4 * h + k, GZ + 4 * h + back, ring_peer(k))

    def along_y(h):
        arrived(gp_in.at[h, 0], GC + 4 * h)
        acc = gp[h, 0, :, mine] + gp_in[h, 0].astype(F32)
        for k in range(1, 4):
            arrived(gz_in.at[h, k], GZ + 4 * h + k)
            acc = acc + gz_in[h, k].astype(F32)
        gy_out[h] = acc.astype(BF16)
        send(gy_out.at[h], gy_in.at[h], GY + h, GY + h, across)

    def to_partner(h):
        arrived(gy_in.at[h], GY + h)
        gf_out[h] = gy_out[h].astype(F32) + gy_in[h].astype(F32)
        send(gf_out.at[h], gf_in.at[h], GF + h, GF + h, partner)
        gproj_ref[:, place(h, core)] = gf_out[h]

    def finish(h):
        arrived(gf_in.at[h], GF + h)
        gproj_ref[:, place(h, 1 - core)] = gf_in[h]

    gather_1(deltas, DT, image_peer, cols[0])
    for s in (1, 2):
        arrived(core_in.at[s], XC + s)
        reduce_3(s, *texts_tree)
    gather_2(deltas, DT, image_peer, cols[0])
    gather_1(deltas, DT + 9, image_peer, cols[1])
    gather_3(deltas, DT, image_peer, cols[0])
    gather_2(deltas, DT + 9, image_peer, cols[1])
    gather_4(deltas, DT, cols[0])
    multiply(0)
    gather_3(deltas, DT + 9, image_peer, cols[1])
    along_z(0)
    gather_4(deltas, DT + 9, cols[1])
    multiply(1)
    along_y(0)
    along_z(1)

    arrived(core_in.at[0], XC + 0)
    total = reduce_4(text_part(0), text_in, XR)
    unit = texts[0:ROWS, :].astype(F32)
    gtext_ref[...] = (total - unit * jnp.sum(unit * total, axis=-1, keepdims=True)) * text_inv
    to_partner(0)
    along_y(1)
    finish(0)
    to_partner(1)
    finish(1)

    for copy in started:
        copy.wait_send()


def on_device(pooled, proj, text, logit_scale, logit_bias):
    vmem = pl.BlockSpec(memory_space=pltpu.VMEM)
    smem = pl.BlockSpec(memory_space=pltpu.SMEM)
    grad_text, grad_proj = pl.pallas_call(
        kernel,
        out_shape=(
            jax.ShapeDtypeStruct((ROWS, EMBED), F32),
            jax.ShapeDtypeStruct((FEATS, EMBED), F32),
        ),
        in_specs=[vmem, pl.BlockSpec(memory_space=pl.ANY), vmem, smem, smem],
        out_specs=(vmem, vmem),
        scratch_shapes=[
            pltpu.VMEM((4 * FEATS, 8 * ROWS), BF16),
            pltpu.VMEM((8, 4 * FEATS, ROWS), BF16),
            pltpu.VMEM((8, 4 * FEATS, EMBED), BF16),
            pltpu.VMEM((8 * ROWS, EMBED), BF16),
            pltpu.VMEM((16 * ROWS, EMBED), BF16),
            pltpu.VMEM((16 * ROWS, EMBED), F32),
            pltpu.VMEM((8 * ROWS, EMBED), BF16),
            pltpu.VMEM((8 * ROWS, EMBED), BF16),
            pltpu.VMEM((8 * ROWS, EMBED), BF16),
            pltpu.VMEM((8, ROWS, EMBED), BF16),
            pltpu.VMEM((8, ROWS, EMBED), BF16),
            pltpu.VMEM((8 * ROWS, EMBED), BF16),
            pltpu.VMEM((8 * ROWS, EMBED), BF16),
            pltpu.VMEM((2, 4, FEATS, HALF), F32),
            pltpu.VMEM((2, 4, FEATS, QUARTER), BF16),
            pltpu.VMEM((2, 4, FEATS, QUARTER), BF16),
            pltpu.VMEM((2, 4, FEATS, QUARTER), BF16),
            pltpu.VMEM((2, 4, FEATS, QUARTER), BF16),
            pltpu.VMEM((2, FEATS, QUARTER), BF16),
            pltpu.VMEM((2, FEATS, QUARTER), BF16),
            pltpu.VMEM((2, FEATS, QUARTER), F32),
            pltpu.VMEM((2, FEATS, QUARTER), F32),
            pltpu.VMEM((8 * ROWS, 16 * ROWS), BF16),
            pltpu.SemaphoreType.DMA((N_SEMS,)),
            pltpu.SemaphoreType.DMA((N_SEMS,)),
            pltpu.SemaphoreType.DMA((8,)),
            pltpu.SemaphoreType.DMA((8, 4)),
        ],
        compiler_params=pltpu.CompilerParams(
            collective_id=0, has_side_effects=True, vmem_limit_bytes=63 * 2**20
        ),
    )(pooled.T, proj, text, logit_scale, logit_bias)
    return (logit_scale[0] * grad_text, logit_scale[0] * grad_proj)


def solution(mesh):
    return jax.shard_map(
        on_device,
        mesh=mesh,
        in_specs=(P("dp", "mp"), P(), P(("dp", "mp"), None), P(), P()),
        out_specs=(P(("dp", "mp"), None), P("mp", None)),
        check_vma=False,
    )
```
